256 devices in a mesh: wide: 32 (over y, z_hi, x), narrow: 8 (over z_lo, core).
Axes of the slice: x: 4, y: 4, z: 8 (z_hi: 2, z_lo: 4; z = z_hi * 4 + z_lo), core: 2. Of those that a mesh axis runs over, the one named last changes fastest.
Arguments:
- tokens: bfloat16 [1024, 8192], P('wide', 'narrow'), may hold values from -6 to 6
- routing: int32 [8], replicated, may hold values from 1 to 1024
- gate_shared: bfloat16 [8192, 29568], P('narrow', 'wide'), may hold values from -0.0625 to 0.0625
- up_shared: bfloat16 [8192, 29568], P('narrow', 'wide'), may hold values from -0.0625 to 0.0625
- down_shared: bfloat16 [29568, 8192], P('wide', 'narrow'), may hold values from -0.03125 to 0.03125
- gate_in: bfloat16 [8192, 8, 128], P('narrow', None, 'wide'), may hold values from -0.5 to 0.5
- gate_out: bfloat16 [8, 128, 29568], P(None, 'narrow', 'wide'), may hold values from -0.0625 to 0.0625
- up_in: bfloat16 [8192, 8, 128], P('narrow', None, 'wide'), may hold values from -0.5 to 0.5
- up_out: bfloat16 [8, 128, 29568], P(None, 'narrow', 'wide'), may hold values from -0.0625 to 0.0625
- down_in: bfloat16 [8, 128, 29568], P(None, 'narrow', 'wide'), may hold values from -0.03125 to 0.03125
- down_out: bfloat16 [8192, 8, 128], P('narrow', None, 'wide'), may hold values from -0.5 to 0.5
Outputs:
- layer_out: bfloat16 [1024, 8192], P('wide', 'narrow')
The draws below stay inside these ranges and needn't reach their ends.
All inputs are finite; a program needn't handle non-finite values.
Results may differ from the reference program's by a relative error of at most 0.03.
Values may be sent and summed in bfloat16 or wider, within the bound.
No kernel may reach another device: no remote copies, remote signals or barrier semaphores. Data moves between devices by JAX's collectives and lax.ppermute only.
A program may use at most 128 MiB of HBM per device.

```python
import jax
import jax.numpy as jnp

D = 8192
FF = 29568
E = 8
R = 128
TOKENS = 1024


def place_ends(entries, own_key, least, high):
    shape = entries.shape
    index_at = [jax.random.randint(jax.random.fold_in(own_key, axis), (), 0, shape[axis]) for axis in range(len(shape))]
    entries = entries.at[tuple(index_at)].set(least)
    longest = shape.index(max(shape))
    index_at[longest] = (index_at[longest] + 1) % shape[longest]
    return entries.at[tuple(index_at)].set(high)


def shard_levels(rng, shape, split, least, top_value):
    level, own = 1.0, jax.random.fold_in(rng, 6)
    for axis_at, parts in split:
        draws = jnp.exp(jax.random.uniform(jax.random.fold_in(own, axis_at), (parts,), jnp.float32, least / len(split), top_value / len(split)))
        level = level * jnp.repeat(draws, shape[axis_at] // parts).reshape([-1 if axis == axis_at else 1 for axis in range(len(shape))])
    return level


def noise(key, extent, spread, reach, shards=(), held_as=jnp.bfloat16):
    values = spread * jax.random.normal(key, extent, jnp.float32)
    if shards:
        values = values * shard_levels(key, extent, shards, -0.22, 0.18)
    return jnp.clip(values, -reach, reach).astype(held_as)


def setup_inputs(seed: int = 0) -> dict:
    splits = jax.random.split(jax.random.key(seed), 12)
    tokens = noise(splits[0], (TOKENS, D), 1.0, 6.0, ((0, 32), (1, 8)))
    routing = place_ends(jax.random.randint(splits[1], (E,), 1, 1025), jax.random.fold_in(splits[1], 1), 1, 1024).astype(jnp.int32)
    gate_shared = noise(splits[2], (D, FF), D ** -0.5, 0.0625, ((0, 8), (1, 32)))
    up_shared = noise(splits[3], (D, FF), D ** -0.5, 0.0625, ((0, 8), (1, 32)))
    down_shared = noise(splits[4], (FF, D), FF ** -0.5, 0.03125, ((0, 32), (1, 8)))
    gate_in = noise(splits[5], (D, E, R), R ** -0.5, 0.5, ((0, 8), (2, 32)))
    gate_out = noise(splits[6], (E, R, FF), D ** -0.5, 0.0625, ((1, 8), (2, 32)))
    up_in = noise(splits[7], (D, E, R), R ** -0.5, 0.5, ((0, 8), (2, 32)))
    up_out = noise(splits[8], (E, R, FF), D ** -0.5, 0.0625, ((1, 8), (2, 32)))
    down_in = noise(splits[9], (E, R, FF), FF ** -0.5, 0.03125, ((1, 8), (2, 32)))
    down_out = noise(splits[10], (D, E, R), R ** -0.5, 0.5, ((0, 8), (2, 32)))
    return dict(tokens=tokens, routing=routing, gate_shared=gate_shared, up_shared=up_shared, down_shared=down_shared, gate_in=gate_in, gate_out=gate_out, up_in=up_in, up_out=up_out, down_in=down_in, down_out=down_out)


def scale_factor(factor, mixing):
    scaled = (factor.astype(jnp.float32) * mixing[None, :, None]).astype(jnp.bfloat16)
    return scaled.reshape(D, E * R)


def reference(tokens, routing, gate_shared, up_shared, down_shared, gate_in, gate_out, up_in, up_out, down_in, down_out):
    mixing = routing.astype(jnp.float32) / 1024.0
    gate_merged = (gate_shared.astype(jnp.float32) + jnp.dot(scale_factor(gate_in, mixing), gate_out.reshape(E * R, FF), preferred_element_type=jnp.float32)).astype(jnp.bfloat16)
    gate = jnp.dot(tokens, gate_merged, preferred_element_type=jnp.float32)
    up_merged = (up_shared.astype(jnp.float32) + jnp.dot(scale_factor(up_in, mixing), up_out.reshape(E * R, FF), preferred_element_type=jnp.float32)).astype(jnp.bfloat16)
    up_value = jnp.dot(tokens, up_merged, preferred_element_type=jnp.float32)
    hidden = (jax.nn.silu(gate) * up_value).astype(jnp.bfloat16)
    scaled_down = scale_factor(down_out, mixing)
    down_merged = (down_shared.astype(jnp.float32) + jnp.dot(down_in.reshape(E * R, FF).T, scaled_down.T, preferred_element_type=jnp.float32)).astype(jnp.bfloat16)
    return jnp.dot(hidden, down_merged, preferred_element_type=jnp.float32).astype(jnp.bfloat16)
```

```python
import jax
import jax.numpy as jnp
from jax import lax
from jax.sharding import PartitionSpec as P

AXES = ("wide", "narrow")
F32, BF16 = jnp.float32, jnp.bfloat16


def pairs(move):
    table = []
    for wide in range(32):
        y, zh, x = wide // 8, wide // 4 % 2, wide % 4
        for narrow in range(8):
            ty, tzh, tx, tn = move(y, zh, x, narrow)
            table.append((wide * 8 + narrow, ((ty * 2 + tzh) * 4 + tx) * 8 + tn))
    return table


def send_x(a, k):
    return lax.ppermute(a, AXES, pairs(lambda y, zh, x, n: (y, zh, (x + k) % 4, n)))


def send_y(a, k):
    return lax.ppermute(a, AXES, pairs(lambda y, zh, x, n: ((y + k) % 4, zh, x, n)))


def swap_zh(a):
    return lax.ppermute(a, AXES, pairs(lambda y, zh, x, n: (y, 1 - zh, x, n)))


def swap_n(a, k):
    return lax.ppermute(a, AXES, pairs(lambda y, zh, x, n: (y, zh, x, n ^ k)))


def gather4(own, send, at):
    got = [own] + [send(own, 4 - m) for m in (1, 2, 3)]
    ring = jnp.stack(got + got[:3])
    return lax.dynamic_slice_in_dim(ring, (4 - at) % 4, 4, 0)


def pick(a, at):
    return lax.dynamic_index_in_dim(a, at, 0, keepdims=False)


def place(pieces, where):
    out = jnp.zeros((len(pieces),) + pieces[0].shape, pieces[0].dtype)
    for piece, at in zip(pieces, where):
        out = lax.dynamic_update_index_in_dim(out, piece, at, 0)
    return out


def total(parts):
    acc = parts[0].astype(F32)
    for part in parts[1:]:
        acc = acc + part.astype(F32)
    return acc


def scatter4(blocks, send, at):
    own = pick(blocks, at)
    got = [send(pick(blocks, (at + k) % 4), k) for k in (1, 2, 3)]
    return total([own] + got)


def shards(
    tokens,
    routing,
    gate_shared,
    up_shared,
    down_shared,
    gate_in,
    gate_out,
    up_in,
    up_out,
    down_in,
    down_out,
):
    wide, narrow = lax.axis_index("wide"), lax.axis_index("narrow")
    y, zh, x = wide // 8, wide // 4 % 2, wide % 4
    zl, core = narrow // 2, narrow % 2
    mixing = routing.astype(F32) / 1024.0
    rows, width = tokens.shape
    hid = gate_shared.shape[1]
    experts, per = gate_in.shape[1:]
    half = rows // 2
    chunk = rows * 4

    other = swap_zh(tokens)
    both = jnp.where(zh == 0, jnp.stack([tokens, other]), jnp.stack([other, tokens]))
    part_a, part_b = both[:, :half], both[:, half:]
    part_a = gather4(part_a, send_x, x)
    part_b = gather4(part_b, send_y, y)
    part_a = gather4(part_a, send_y, y)
    part_b = gather4(part_b, send_x, x)
    halves = jnp.stack([part_a.reshape(4 * chunk, width), part_b.reshape(4 * chunk, width)])

    def scaled(factor):
        flat = jnp.transpose(factor, (1, 2, 0)).astype(F32) * mixing[:, None, None]
        return flat.astype(BF16).reshape(experts * per, width)

    def by_rank(factor):
        cut = factor.reshape(experts, 4, per, hid)
        return jnp.transpose(cut, (1, 0, 2, 3)).reshape(4 * experts * per, hid)

    side = jnp.concatenate([scaled(gate_in), scaled(up_in)])
    down_side = lax.all_gather(scaled(down_out), "wide", axis=0, tiled=True)
    hid_own = jnp.stack([by_rank(gate_out), by_rank(up_out)])
    hid_col = place([hid_own] + [swap_n(hid_own, 2 * k) for k in (1, 2, 3)], [zl ^ k for k in range(4)])
    hid_other = swap_n(hid_col, 1)
    hid_side = jnp.where(core == 0, jnp.stack([hid_col, hid_other], 1), jnp.stack([hid_other, hid_col], 1))

    def by_feature(a, b):
        return lax.dot_general(a, b, (((1,), (1,)), ((), ())), preferred_element_type=F32)

    keep, give = pick(halves, core), pick(halves, 1 - core)
    low_give = swap_n(by_feature(side, give).astype(BF16), 1)
    low = (by_feature(side, keep) + low_give.astype(F32)).astype(BF16)
    low = jnp.transpose(low.reshape(-1, 4, chunk), (1, 0, 2))
    low = total([pick(low, zl)] + [swap_n(pick(low, zl ^ k), 2 * k) for k in (1, 2, 3)]).astype(BF16)
    low_other = swap_zh(low)
    low = jnp.where(zh == 0, jnp.stack([low, low_other]), jnp.stack([low_other, low]))
    low_gate, low_up = low[:, : experts * per], low[:, experts * per :]
    low_gate = gather4(low_gate, send_x, x)
    low_up = gather4(low_up, send_y, y)
    low_gate = jnp.transpose(gather4(low_gate, send_y, y), (0, 2, 1, 3, 4))
    low_up = jnp.transpose(gather4(low_up, send_x, x), (1, 2, 0, 3, 4))
    low_gate = low_gate.reshape(-1, chunk)
    low_up = low_up.reshape(-1, chunk)

    def by_width(a, b):
        return lax.dot_general(a, b, (((0,), (1,)), ((), ())), preferred_element_type=F32)

    def first(block):
        return jnp.stack([by_width(gate_shared, block), by_width(up_shared, block)])

    sums = first(keep) + swap_n(first(give).astype(BF16), 1).astype(F32)
    sums = jnp.transpose(sums.astype(BF16).reshape(2, hid, 4, chunk), (2, 0, 1, 3))
    sums = total([pick(sums, zl)] + [swap_n(pick(sums, zl ^ k), 2 * k) for k in (1, 2, 3)])

    def by_rows(a, b):
        return lax.dot_general(a, b, (((0,), (0,)), ((), ())), preferred_element_type=F32)

    gate = sums[0] + by_rows(hid_side[:, :, 0].reshape(-1, hid), low_gate)
    up = sums[1] + by_rows(hid_side[:, :, 1].reshape(-1, hid), low_up)
    hidden = (jax.nn.silu(gate) * up).astype(BF16)

    column = place([hidden] + [swap_n(hidden, 2 * k) for k in (1, 2, 3)], [zl ^ k for k in range(4)])
    sibling = swap_n(column, 1)
    hidden_a = jnp.where(core == 0, column, sibling)
    hidden_b = jnp.where(core == 0, sibling, column)

    down_hid = by_rank(down_in)

    def last(block):
        base = jnp.einsum("qft,fd->qtd", block, down_shared, preferred_element_type=F32)
        low_rank = jnp.einsum("qft,rf->qtr", block, down_hid, preferred_element_type=F32)
        return jnp.concatenate([base, low_rank], axis=2).astype(BF16)

    out_a, out_b = last(hidden_a), last(hidden_b)
    out_a = scatter4(out_a, send_y, y).astype(BF16).reshape(4, 2 * half, -1)
    out_b = scatter4(out_b, send_x, x).astype(BF16).reshape(4, 2 * half, -1)
    out_a = scatter4(out_a, send_x, x).astype(BF16).reshape(2, half, -1)
    out_b = scatter4(out_b, send_y, y).astype(BF16).reshape(2, half, -1)
    out = jnp.concatenate([out_a, out_b], axis=1)
    out = pick(out, zh).astype(F32) + swap_zh(pick(out, 1 - zh)).astype(F32)
    mine = out[:, width:].astype(BF16)
    ranks = place([mine] + [swap_n(mine, k) for k in range(1, 8)], [narrow ^ k for k in range(8)])
    update = jnp.einsum(
        "ntr,nrd->td", ranks, down_side.reshape(8, -1, width), preferred_element_type=F32
    )
    return (out[:, :width] + update).astype(BF16)


def solution(mesh):
    return jax.shard_map(
        shards,
        mesh=mesh,
        in_specs=(
            P("wide", "narrow"),
            P(),
            P("narrow", "wide"),
            P("narrow", "wide"),
            P("wide", "narrow"),
            P("narrow", None, "wide"),
            P(None, "narrow", "wide"),
            P("narrow", None, "wide"),
            P(None, "narrow", "wide"),
            P(None, "narrow", "wide"),
            P("narrow", None, "wide"),
        ),
        out_specs=P("wide", "narrow"),
        check_vma=False,
    )
```

```python
import functools

import jax
import jax.numpy as jnp
from jax import lax
from jax.experimental import pallas as pl
from jax.experimental.pallas import tpu as pltpu
from jax.sharding import PartitionSpec as P

AXES = ("wide", "narrow")
F32, BF16 = jnp.float32, jnp.bfloat16
VMEM_LIMIT = 14 * 1024 * 1024


def pairs(move):
    table = []
    for wide in range(32):
        y, zh, x = wide // 8, wide // 4 % 2, wide % 4
        for narrow in range(8):
            ty, tzh, tx, tn = move(y, zh, x, narrow)
            table.append((wide * 8 + narrow, ((ty * 2 + tzh) * 4 + tx) * 8 + tn))
    return table


def send_x(a, k):
    return lax.ppermute(a, AXES, pairs(lambda y, zh, x, n: (y, zh, (x + k) % 4, n)))


def send_y(a, k):
    return lax.ppermute(a, AXES, pairs(lambda y, zh, x, n: ((y + k) % 4, zh, x, n)))


def swap_zh(a):
    return lax.ppermute(a, AXES, pairs(lambda y, zh, x, n: (y, 1 - zh, x, n)))


def swap_n(a, k):
    return lax.ppermute(a, AXES, pairs(lambda y, zh, x, n: (y, zh, x, n ^ k)))


def after(a, *others):
    return lax.optimization_barrier((a,) + others)[0]


def gather4(own, send, at):
    got = [own] + [send(own, 4 - m) for m in (1, 2, 3)]
    ring = jnp.stack(got + got[:3])
    return lax.dynamic_slice_in_dim(ring, (4 - at) % 4, 4, 0)


def pieces4(own, send):
    return [own] + [send(own, k) for k in (1, 2, 3)]


def pick(a, at):
    return lax.dynamic_index_in_dim(a, at, 0, keepdims=False)


def contract(a, b, da, db):
    return lax.dot_general(a, b, (((da,), (db,)), ((), ())), preferred_element_type=F32)


def padded(rows, unit=16):
    return (rows + unit - 1) // unit * unit


def pad_rows(a, unit=16):
    rows = a.shape[-2]
    return jnp.pad(a, [(0, 0)] * (a.ndim - 2) + [(0, padded(rows, unit) - rows), (0, 0)])


def whole(a):
    zeros = (0,) * a.ndim
    return pl.BlockSpec(a.shape, lambda i, where: zeros)


HERE = pl.BlockSpec(memory_space=pl.ANY)


def in_hbm(arrays):
    return [pltpu.with_memory_space_constraint(a, pltpu.HBM) for a in arrays]


def call(body, where, grid, ins, in_specs, outs, out_specs, scratch, flops):
    moved = sum(a.size * a.dtype.itemsize for a in list(ins) + list(outs))
    return pl.pallas_call(
        body,
        out_shape=outs,
        grid_spec=pltpu.PrefetchScalarGridSpec(
            num_scalar_prefetch=1,
            grid=(grid,),
            in_specs=in_specs,
            out_specs=out_specs,
            scratch_shapes=scratch,
        ),
        compiler_params=pltpu.CompilerParams(vmem_limit_bytes=VMEM_LIMIT),
        cost_estimate=pl.CostEstimate(flops=flops, bytes_accessed=moved, transcendentals=0),
    )(where, *ins)


def fetch(where, half, a, b, toks, sems, slot_of):
    pos = jnp.where(half == 0, where[3], where[5])
    chunk = a[0].shape[0]
    for k in range(4):
        slot, wanted = slot_of(((pos + 4 - k) % 4) ^ where[2])
        rows = toks.at[pl.ds(pl.multiple_of(slot * chunk, chunk), chunk), :]
        for at, pieces in ((0, a), (1, b)):

            @pl.when((half == at) & wanted)
            def _():
                pltpu.make_async_copy(pieces[k], rows, sems.at[slot]).start()


def arrived(a, toks, sems, slots):
    chunk = a[0].shape[0]
    for slot in range(slots):
        rows = toks.at[pl.ds(slot * chunk, chunk), :]
        pltpu.make_async_copy(a[0], rows, sems.at[slot]).wait()


def low_body(where, *refs):
    a, b = refs[:4], refs[4:8]
    side, give, keep, toks, sems = refs[8:]
    chunk = a[0].shape[0]
    halves = ((1 - where[1], give, 0), (where[1], keep, 4))
    for half, _, base in halves:
        fetch(where, half, a, b, toks, sems, lambda near: (near + base, True))
    arrived(a, toks, sems, 8)
    for _, out, base in halves:
        rows = slice(base * chunk, (base + 4) * chunk)
        sums = contract(side[...], toks[rows, :], 1, 1)
        for k in range(4):
            out[k] = sums[:, k * chunk : (k + 1) * chunk].astype(BF16)


def low_rank(where, a, b, side):
    chunk, width = a[0].shape
    out = jax.ShapeDtypeStruct((4, side.shape[0], chunk), BF16)
    return call(
        low_body,
        where,
        1,
        [*a, *b, side],
        [HERE] * 8 + [whole(side)],
        [out, out],
        [whole(out), whole(out)],
        [pltpu.VMEM((8 * chunk, width), BF16), pltpu.SemaphoreType.DMA((8,))],
        16 * side.shape[0] * width * chunk,
    )


def first_body(where, *refs):
    a, b = refs[:4], refs[4:8]
    gate, up, out, toks, sems = refs[8:]
    chunk = a[0].shape[0]

    @pl.when(pl.program_id(0) == 0)
    def _():
        fetch(where, where[0], a, b, toks, sems, lambda near: (1 - near % 2, near // 2 == where[7]))
        arrived(a, toks, sems, 2)

    for g, weight in enumerate((gate, up)):
        sums = contract(weight[...], toks[...], 1, 1)
        for slot in range(2):
            out[slot, g] = sums[:, slot * chunk : (slot + 1) * chunk].astype(BF16)


def first(where, a, b, gate, up):
    hid, width = gate.shape
    chunk = a[0].shape[0]
    tile = 464
    weight = pl.BlockSpec((tile, width), lambda i, where: (i, 0))
    return call(
        first_body,
        where,
        pl.cdiv(hid, tile),
        [*a, *b, gate, up],
        [HERE] * 8 + [weight, weight],
        [jax.ShapeDtypeStruct((2, 2, padded(hid), chunk), BF16)],
        [pl.BlockSpec((2, 2, tile, chunk), lambda i, where: (0, 0, i, 0))],
        [pltpu.VMEM((2 * chunk, width), BF16), pltpu.SemaphoreType.DMA((2,))],
        8 * hid * width * chunk,
    )[0]


def arrange(where, blocks, store):
    y, zh, x = where[3], where[4], where[5]
    for ky in range(4):
        for kz in range(2):
            n = ((y + 4 - ky) % 4) * 2 + (zh ^ kz)
            for kx in range(4):
                store(n, (x + kx) % 4, blocks[ky][kz, kx])


def mid_body(hid, where, *refs):
    keep, recv = refs[:2]
    got, fac, low = refs[2:4], refs[4], refs[5:9]
    out, ranks = refs[9:]
    per = ranks.shape[3]

    @pl.when(pl.program_id(0) == 0)
    def _():
        def store(n, xs, block):
            for g in range(2):
                ranks[g, n, xs] = block[g * per : (g + 1) * per, :]

        arrange(where, low, store)

    values = []
    for g in range(2):
        acc = keep[0, g].astype(F32) + recv[0, g].astype(F32)
        for part in got:
            acc = acc + part[g].astype(F32)
        side = jnp.concatenate([fac[k, g] for k in range(8)], axis=1)
        values.append(acc + contract(side, ranks[g].reshape(-1, ranks.shape[4]), 1, 0))
    gate, up = values
    value = gate / (1.0 + jnp.exp(-gate)) * up
    row = pl.program_id(0) * out.shape[0] + lax.broadcasted_iota(jnp.int32, value.shape, 0)
    out[...] = jnp.where(row < hid, value, 0.0).astype(BF16)


def middle(where, keep, recv, got, fac, low, used):
    _, _, hid, chunk = keep.shape
    tile = 256
    full = pl.BlockSpec((1, 2, tile, chunk), lambda i, where: (1, 0, i, 0))
    part = pl.BlockSpec((2, tile, chunk), lambda i, where: (0, i, 0))
    factor = pl.BlockSpec((8, 2, tile, fac.shape[3]), lambda i, where: (0, 0, i, 0))
    return call(
        functools.partial(mid_body, used),
        where,
        pl.cdiv(hid, tile),
        [keep, recv, *got, *in_hbm([fac]), *low],
        [full, full] + [part] * 2 + [factor] + [whole(p) for p in low],
        [jax.ShapeDtypeStruct((hid, chunk), BF16)],
        [pl.BlockSpec((tile, chunk), lambda i, where: (i, 0))],
        [pltpu.VMEM((2, 8, 4, low[0].shape[2] // 2, chunk), BF16)],
        32 * fac.shape[3] * hid * chunk,
    )[0]


def last_body(where, *refs):
    own, sib, weight = refs[:4], refs[4:8], refs[8]
    outs, hidden, sems = refs[9:17], refs[17], refs[18]
    core, zl = where[1], where[2]
    chunk = hidden.shape[2]

    @pl.when(pl.program_id(0) == 0)
    def _():
        copies = []
        for at, pieces in ((core, own), (1 - core, sib)):
            pos = jnp.where(at == 0, where[3], where[5])
            for k in range(4):
                slot = hidden.at[at * 4 + ((zl ^ k) + 4 - pos) % 4]
                copies.append(pltpu.make_async_copy(pieces[k], slot, sems.at[len(copies)]))
                copies[-1].start()
        for copy in copies:
            copy.wait()

    left = jnp.concatenate([hidden[k] for k in range(8)], axis=1)
    sums = contract(left, weight[...], 0, 0)
    for k in range(8):
        outs[k][...] = sums[k * chunk : (k + 1) * chunk].astype(BF16)


def last(where, own, sib, weight):
    hid, chunk = own[0].shape
    cols = weight.shape[1]
    tile = 384 if cols % 384 == 0 else cols
    outs = call(
        last_body,
        where,
        cols // tile,
        [*own, *sib, weight],
        [HERE] * 8 + [pl.BlockSpec((hid, tile), lambda i, where: (0, i))],
        [jax.ShapeDtypeStruct((chunk, cols), BF16)] * 8,
        [pl.BlockSpec((chunk, tile), lambda i, where: (0, i))] * 8,
        [pltpu.VMEM((8, hid, chunk), BF16), pltpu.SemaphoreType.DMA((8,))],
        16 * chunk * hid * cols,
    )
    return outs[:4], outs[4:]


def add4(parts, rows):
    acc = parts[0][rows, :].astype(F32)
    for part in parts[1:]:
        acc = acc + part[rows, :].astype(F32)
    return acc


def split_body(where, *refs):
    size = refs[8].shape[0]
    for parts, outs, pos in ((refs[:4], refs[8:12], where[5]), (refs[4:8], refs[12:16], where[3])):
        for k in range(4):
            start = pl.multiple_of((pos + k) % 4 * size, size)
            outs[k][...] = add4(parts, pl.ds(start, size)).astype(BF16)


def split(where, a, b):
    rows, cols = a[0].shape
    outs = [jax.ShapeDtypeStruct((rows // 4, cols), BF16)] * 8
    outs = call(split_body, where, 1, [*a, *b], [whole(p) for p in [*a, *b]], outs, [whole(p) for p in outs], [], 0)
    return outs[:4], outs[4:]


def halve_body(where, *refs):
    keep, give = refs[8:]
    size = keep.shape[0] // 2
    for h in range(2):
        parts = refs[4 * h : 4 * h + 4]
        for out, at in ((keep, where[4]), (give, 1 - where[4])):
            start = pl.multiple_of(at * size, size)
            out[h * size : (h + 1) * size, :] = add4(parts, pl.ds(start, size)).astype(out.dtype)


def halve(where, a, b):
    outs = [jax.ShapeDtypeStruct(a[0].shape, F32), jax.ShapeDtypeStruct(a[0].shape, BF16)]
    return call(halve_body, where, 1, [*a, *b], [whole(p) for p in [*a, *b]], outs, [whole(p) for p in outs], [], 0)


def end_body(where, *refs):
    keep, recv, low, side = refs[0], refs[1], refs[2:6], refs[6:10]
    out, ranks = refs[10:]
    y, zh, x, narrow = where[3], where[4], where[5], where[6]
    per = side[0].shape[2]

    @pl.when(pl.program_id(0) == 0)
    def _():
        for k in range(8):
            ranks[k] = low[k // 2][k % 2].astype(F32)

    acc = keep[...] + recv[...].astype(F32)
    for ky in range(4):
        for kz in range(2):
            n = ((y + 4 - ky) % 4) * 2 + (zh ^ kz)
            left = pltpu.roll(ranks[narrow ^ n], (4 - x) % 4 * per, 1).astype(BF16)
            acc = acc + contract(left, side[ky][kz].reshape(4 * per, -1), 1, 0)
    out[...] = acc.astype(BF16)


def end(where, keep, recv, low, side):
    rows = keep.shape[0]
    _, _, per, width = side[0].shape
    tile = 512 if width % 512 == 0 else width
    column = pl.BlockSpec((rows, tile), lambda i, where: (0, i))
    block = pl.BlockSpec((2, 4, per, tile), lambda i, where: (0, 0, 0, i))
    return call(
        end_body,
        where,
        width // tile,
        [keep, recv, *low, *side],
        [column, column] + [whole(u) for u in low] + [block] * 4,
        [jax.ShapeDtypeStruct((rows, width), BF16)],
        [column],
        [pltpu.VMEM((8, rows, 4 * per), F32)],
        64 * rows * per * width,
    )[0]


def shards(
    tokens,
    routing,
    gate_shared,
    up_shared,
    down_shared,
    gate_in,
    gate_out,
    up_in,
    up_out,
    down_in,
    down_out,
):
    wide, narrow = lax.axis_index("wide"), lax.axis_index("narrow")
    y, zh, x = wide // 8, wide // 4 % 2, wide % 4
    zl, core = narrow // 2, narrow % 2

    def where(half, side=0):
        return jnp.stack([half, core, zl, y, zh, x, narrow, core * 0 + side]).astype(jnp.int32)

    mixing = routing.astype(F32) / 1024.0
    rows, width = tokens.shape
    hid = gate_shared.shape[1]
    experts, per = gate_in.shape[1:]
    half = rows // 2
    chunk = rows * 4

    def turned(factor):
        return jnp.transpose(factor, (1, 2, 0))

    def scaled(factor):
        flat = factor.astype(F32) * mixing[:, None, None]
        return flat.astype(BF16).reshape(experts * per, width)

    def by_rank(factor):
        cut = factor.reshape(experts, 4, per, hid)
        return jnp.transpose(cut, (1, 0, 2, 3)).reshape(4 * experts * per, hid)

    down_own = scaled(turned(down_out))
    other = swap_zh(jnp.concatenate([tokens, down_own]))
    down_pair = jnp.stack([down_own, other[rows:]])
    other = other[:rows]
    both = jnp.where(zh == 0, jnp.stack([tokens, other]), jnp.stack([other, tokens]))
    part_a = gather4(both[:, :half], send_x, x).reshape(chunk, width)
    part_b = gather4(both[:, half:], send_y, y).reshape(chunk, width)
    side = jnp.concatenate([scaled(turned(gate_in)), scaled(turned(up_in))])
    part_a, part_b, side, down_pair = lax.optimization_barrier((part_a, part_b, side, down_pair))
    toks_a = pieces4(part_a, send_y)
    toks_b = pieces4(part_b, send_x)

    out_g, out_u, _ = lax.optimization_barrier((gate_out, up_out, other))
    hid_own = pad_rows(jnp.stack([by_rank(out_g).T, by_rank(out_u).T]))
    hid_fac = lax.all_gather(hid_own, "narrow")
    weight = pad_rows(jnp.concatenate([down_shared, by_rank(down_in).T], axis=1))

    low_give, low_keep = low_rank(where(core), toks_a, toks_b, side)
    low_recv = swap_n(low_give, 1)

    def joined(a, b, slot):
        return a[slot].astype(F32) + b[slot].astype(F32)

    args = (toks_a, toks_b, gate_shared.T, up_shared.T)
    give = first(after(where(1 - core, 1), low_give), *args)
    recv = swap_n(give, 1)
    low = joined(low_keep, low_recv, 0)
    for k in (3, 2, 1):
        low = low + swap_n(joined(low_keep, low_recv, k).astype(BF16), 2 * k).astype(F32)
    low = low.astype(BF16)
    keep = first(where(core, 1), *args)
    low_other = swap_zh(low)
    cross_in = joined(keep, recv, 0).astype(BF16)

    def line(pair):
        return jnp.stack([pair] + [send_x(pair, 4 - m) for m in (1, 2, 3)], axis=1)

    cross = swap_n(after(cross_in, low_other), 2)

    give = first(after(where(1 - core, 0), cross_in), *args)
    near_recv = swap_n(give, 1)
    near_keep = first(after(where(core, 0), give), *args)
    far = (joined(keep, recv, 1) + cross.astype(F32)).astype(BF16)
    near = swap_n(after(joined(near_keep, near_recv, 0).astype(BF16), cross), 2)
    got = [near, swap_n(far, 4)]

    low_line = line(jnp.stack([low, low_other]))
    low = pieces4(low_line, send_y)
    down_line = line(after(down_pair, far))
    down_side = [down_line, send_y(down_line, 1), None, send_y(down_line, 3)]
    near_keep = after(near_keep, down_side[1], down_side[3])
    hidden = middle(where(core), near_keep, near_recv, got, hid_fac, low, hid)
    down_side[2] = send_y(after(down_line, hidden), 2)

    column = [hidden] + [swap_n(hidden, 2 * k) for k in (1, 2, 3)]
    sibling = [swap_n(piece, 1) for piece in column]

    column[0] = after(column[0], down_side[2])
    out_a, out_b = last(where(core), column, sibling, weight)
    out_a = [out_a[0]] + [send_y(out_a[k], k) for k in (1, 2, 3)]
    out_b = [out_b[0]] + [send_x(out_b[k], k) for k in (1, 2, 3)]
    out_a, out_b = split(where(core), out_a, out_b)
    out_a = [out_a[0]] + [send_x(out_a[k], k) for k in (1, 2, 3)]
    out_b = [out_b[0]] + [send_y(out_b[k], k) for k in (1, 2, 3)]
    kept, give = halve(where(core), out_a, out_b)
    recv = swap_zh(give)
    mine = (kept[:, width:] + recv[:, width:].astype(F32)).astype(BF16)
    mine = jnp.stack([mine, swap_n(mine, 1)])
    ranks = [mine] + [swap_n(mine, 2 * k) for k in (1, 2, 3)]
    return end(where(core), kept, recv, ranks, down_side)


def solution(mesh):
    return jax.shard_map(
        shards,
        mesh=mesh,
        in_specs=(
            P("wide", "narrow"),
            P(),
            P("narrow", "wide"),
            P("narrow", "wide"),
            P("wide", "narrow"),
            P("narrow", None, "wide"),
            P(None, "narrow", "wide"),
            P("narrow", None, "wide"),
            P(None, "narrow", "wide"),
            P(None, "narrow", "wide"),
            P("narrow", None, "wide"),
        ),
        out_specs=P("wide", "narrow"),
        check_vma=False,
    )
```

```python
import functools

import jax
import jax.numpy as jnp
from jax import lax
from jax.experimental import pallas as pl
from jax.experimental.pallas import tpu as pltpu
from jax.sharding import PartitionSpec as P

AXES = ("wide", "narrow")
F32, BF16 = jnp.float32, jnp.bfloat16
VMEM_LIMIT = 14 * 1024 * 1024


def pairs(move):
    table = []
    for wide in range(32):
        y, zh, x = wide // 8, wide // 4 % 2, wide % 4
        for narrow in range(8):
            ty, tzh, tx, tn = move(y, zh, x, narrow)
            table.append((wide * 8 + narrow, ((ty * 2 + tzh) * 4 + tx) * 8 + tn))
    return table


def send_x(a, k):
    return lax.ppermute(a, AXES, pairs(lambda y, zh, x, n: (y, zh, (x + k) % 4, n)))


def send_y(a, k):
    return lax.ppermute(a, AXES, pairs(lambda y, zh, x, n: ((y + k) % 4, zh, x, n)))


def swap_zh(a):
    return lax.ppermute(a, AXES, pairs(lambda y, zh, x, n: (y, 1 - zh, x, n)))


def swap_n(a, k):
    return lax.ppermute(a, AXES, pairs(lambda y, zh, x, n: (y, zh, x, n ^ k)))


def after(a, *others):
    return lax.optimization_barrier((a,) + others)[0]


def gather4(own, send, at):
    got = [own] + [send(own, 4 - m) for m in (1, 2, 3)]
    ring = jnp.stack(got + got[:3])
    return lax.dynamic_slice_in_dim(ring, (4 - at) % 4, 4, 0)


def pieces4(own, send):
    return [own] + [send(own, k) for k in (1, 2, 3)]


def pick(a, at):
    return lax.dynamic_index_in_dim(a, at, 0, keepdims=False)


def contract(a, b, da, db):
    return lax.dot_general(a, b, (((da,), (db,)), ((), ())), preferred_element_type=F32)


def padded(rows, unit=16):
    return (rows + unit - 1) // unit * unit


def pad_rows(a, unit=16):
    rows = a.shape[-2]
    return jnp.pad(a, [(0, 0)] * (a.ndim - 2) + [(0, padded(rows, unit) - rows), (0, 0)])


def whole(a):
    zeros = (0,) * a.ndim
    return pl.BlockSpec(a.shape, lambda i, where: zeros)


HERE = pl.BlockSpec(memory_space=pl.ANY)


def in_hbm(arrays):
    return [pltpu.with_memory_space_constraint(a, pltpu.HBM) for a in arrays]


def call(body, where, grid, ins, in_specs, outs, out_specs, scratch, flops):
    moved = sum(a.size * a.dtype.itemsize for a in list(ins) + list(outs))
    return pl.pallas_call(
        body,
        out_shape=outs,
        grid_spec=pltpu.PrefetchScalarGridSpec(
            num_scalar_prefetch=1,
            grid=(grid,),
            in_specs=in_specs,
            out_specs=out_specs,
            scratch_shapes=scratch,
        ),
        compiler_params=pltpu.CompilerParams(vmem_limit_bytes=VMEM_LIMIT),
        cost_estimate=pl.CostEstimate(flops=flops, bytes_accessed=moved, transcendentals=0),
    )(where, *ins)


def fetch(where, half, a, b, toks, sems, slot_of):
    pos = jnp.where(half == 0, where[3], where[5])
    chunk = a[0].shape[0]
    for k in range(4):
        slot, wanted = slot_of(((pos + 4 - k) % 4) ^ where[2])
        rows = toks.at[pl.ds(pl.multiple_of(slot * chunk, chunk), chunk), :]
        for at, pieces in ((0, a), (1, b)):

            @pl.when((half == at) & wanted)
            def _():
                pltpu.make_async_copy(pieces[k], rows, sems.at[slot]).start()


def arrived(a, toks, sems, slots):
    chunk = a[0].shape[0]
    for slot in range(slots):
        rows = toks.at[pl.ds(slot * chunk, chunk), :]
        pltpu.make_async_copy(a[0], rows, sems.at[slot]).wait()


def low_body(where, *refs):
    a, b = refs[:4], refs[4:8]
    side, give, keep, toks, sems = refs[8:]
    chunk = a[0].shape[0]
    halves = ((1 - where[1], give, 0), (where[1], keep, 4))
    for half, _, base in halves:
        fetch(where, half, a, b, toks, sems, lambda near: (near + base, True))
    arrived(a, toks, sems, 8)
    for _, out, base in halves:
        rows = slice(base * chunk, (base + 4) * chunk)
        sums = contract(side[...], toks[rows, :], 1, 1)
        for k in range(4):
            out[k] = sums[:, k * chunk : (k + 1) * chunk].astype(BF16)


def low_rank(where, a, b, side):
    chunk, width = a[0].shape
    out = jax.ShapeDtypeStruct((4, side.shape[0], chunk), BF16)
    return call(
        low_body,
        where,
        1,
        [*a, *b, side],
        [HERE] * 8 + [whole(side)],
        [out, out],
        [whole(out), whole(out)],
        [pltpu.VMEM((8 * chunk, width), BF16), pltpu.SemaphoreType.DMA((8,))],
        16 * side.shape[0] * width * chunk,
    )


def first_body(where, *refs):
    a, b = refs[:4], refs[4:8]
    gate, up, out, toks, sems = refs[8:]
    chunk = a[0].shape[0]

    @pl.when(pl.program_id(0) == 0)
    def _():
        fetch(where, where[0], a, b, toks, sems, lambda near: (1 - near % 2, near // 2 == where[7]))
        arrived(a, toks, sems, 2)

    for g, weight in enumerate((gate, up)):
        sums = contract(weight[...], toks[...], 1, 1)
        for slot in range(2):
            out[slot, g] = sums[:, slot * chunk : (slot + 1) * chunk].astype(BF16)


def first(where, a, b, gate, up):
    hid, width = gate.shape
    chunk = a[0].shape[0]
    tile = 464
    weight = pl.BlockSpec((tile, width), lambda i, where: (i, 0))
    return call(
        first_body,
        where,
        pl.cdiv(hid, tile),
        [*a, *b, gate, up],
        [HERE] * 8 + [weight, weight],
        [jax.ShapeDtypeStruct((2, 2, padded(hid), chunk), BF16)],
        [pl.BlockSpec((2, 2, tile, chunk), lambda i, where: (0, 0, i, 0))],
        [pltpu.VMEM((2 * chunk, width), BF16), pltpu.SemaphoreType.DMA((2,))],
        8 * hid * width * chunk,
    )[0]


def arrange(where, blocks, store):
    y, zh, x = where[3], where[4], where[5]
    for ky in range(4):
        for kz in range(2):
            n = ((y + 4 - ky) % 4) * 2 + (zh ^ kz)
            for kx in range(4):
                store(n, (x + kx) % 4, blocks[ky][kz, kx])


def mid_body(hid, where, *refs):
    keep, recv = refs[:2]
    got, fac, low = refs[2:4], refs[4], refs[5:9]
    out, ranks = refs[9:]
    per = ranks.shape[3]

    @pl.when(pl.program_id(0) == 0)
    def _():
        def store(n, xs, block):
            for g in range(2):
                ranks[g, n, xs] = block[g * per : (g + 1) * per, :]

        arrange(where, low, store)

    values = []
    for g in range(2):
        acc = keep[0, g].astype(F32) + recv[0, g].astype(F32)
        for part in got:
            acc = acc + part[g].astype(F32)
        side = jnp.concatenate([fac[k, g] for k in range(8)], axis=1)
        values.append(acc + contract(side, ranks[g].reshape(-1, ranks.shape[4]), 1, 0))
    gate, up = values
    value = gate / (1.0 + jnp.exp(-gate)) * up
    row = pl.program_id(0) * out.shape[0] + lax.broadcasted_iota(jnp.int32, value.shape, 0)
    out[...] = jnp.where(row < hid, value, 0.0).astype(BF16)


def middle(where, keep, recv, got, fac, low, used):
    _, _, hid, chunk = keep.shape
    tile = 256
    full = pl.BlockSpec((1, 2, tile, chunk), lambda i, where: (1, 0, i, 0))
    part = pl.BlockSpec((2, tile, chunk), lambda i, where: (0, i, 0))
    factor = pl.BlockSpec((8, 2, tile, fac.shape[3]), lambda i, where: (0, 0, i, 0))
    return call(
        functools.partial(mid_body, used),
        where,
        pl.cdiv(hid, tile),
        [*in_hbm([keep, recv]), *got, *in_hbm([fac, *low])],
        [full, full] + [part] * 2 + [factor] + [whole(p) for p in low],
        [jax.ShapeDtypeStruct((hid, chunk), BF16)],
        [pl.BlockSpec((tile, chunk), lambda i, where: (i, 0))],
        [pltpu.VMEM((2, 8, 4, low[0].shape[2] // 2, chunk), BF16)],
        32 * fac.shape[3] * hid * chunk,
    )[0]


def last_body(where, *refs):
    own, sib, weight = refs[:4], refs[4:8], refs[8]
    outs, hidden, sems = refs[9:17], refs[17], refs[18]
    core, zl = where[1], where[2]
    chunk = hidden.shape[2]

    @pl.when(pl.program_id(0) == 0)
    def _():
        copies = []
        for at, pieces in ((core, own), (1 - core, sib)):
            pos = jnp.where(at == 0, where[3], where[5])
            for k in range(4):
                slot = hidden.at[at * 4 + ((zl ^ k) + 4 - pos) % 4]
                copies.append(pltpu.make_async_copy(pieces[k], slot, sems.at[len(copies)]))
                copies[-1].start()
        for copy in copies:
            copy.wait()

    left = jnp.concatenate([hidden[k] for k in range(8)], axis=1)
    sums = contract(left, weight[...], 0, 0)
    for k in range(8):
        outs[k][...] = sums[k * chunk : (k + 1) * chunk].astype(BF16)


def last(where, own, sib, weight):
    hid, chunk = own[0].shape
    cols = weight.shape[1]
    tile = 384 if cols % 384 == 0 else cols
    outs = call(
        last_body,
        where,
        cols // tile,
        [*own, *sib, weight],
        [HERE] * 8 + [pl.BlockSpec((hid, tile), lambda i, where: (0, i))],
        [jax.ShapeDtypeStruct((chunk, cols), BF16)] * 8,
        [pl.BlockSpec((chunk, tile), lambda i, where: (0, i))] * 8,
        [pltpu.VMEM((8, hid, chunk), BF16), pltpu.SemaphoreType.DMA((8,))],
        16 * chunk * hid * cols,
    )
    return outs[:4], outs[4:]


def add4(parts, rows):
    acc = parts[0][rows, :].astype(F32)
    for part in parts[1:]:
        acc = acc + part[rows, :].astype(F32)
    return acc


def split_body(where, *refs):
    size = refs[8].shape[0]
    for parts, outs, pos in ((refs[:4], refs[8:12], where[5]), (refs[4:8], refs[12:16], where[3])):
        for k in range(4):
            start = pl.multiple_of((pos + k) % 4 * size, size)
            outs[k][...] = add4(parts, pl.ds(start, size)).astype(BF16)


def split(where, a, b):
    rows, cols = a[0].shape
    outs = [jax.ShapeDtypeStruct((rows // 4, cols), BF16)] * 8
    outs = call(split_body, where, 1, [*a, *b], [whole(p) for p in [*a, *b]], outs, [whole(p) for p in outs], [], 0)
    return outs[:4], outs[4:]


def halve_body(where, *refs):
    keep, give = refs[8:]
    size = keep.shape[0] // 2
    for h in range(2):
        parts = refs[4 * h : 4 * h + 4]
        for out, at in ((keep, where[4]), (give, 1 - where[4])):
            start = pl.multiple_of(at * size, size)
            out[h * size : (h + 1) * size, :] = add4(parts, pl.ds(start, size)).astype(out.dtype)


def halve(where, a, b):
    outs = [jax.ShapeDtypeStruct(a[0].shape, F32), jax.ShapeDtypeStruct(a[0].shape, BF16)]
    return call(halve_body, where, 1, [*a, *b], [whole(p) for p in [*a, *b]], outs, [whole(p) for p in outs], [], 0)


def end_body(where, *refs):
    keep, recv, low, side = refs[0], refs[1], refs[2:6], refs[6:10]
    out, ranks = refs[10:]
    y, zh, x, narrow = where[3], where[4], where[5], where[6]
    per = side[0].shape[2]

    @pl.when(pl.program_id(0) == 0)
    def _():
        for k in range(8):
            ranks[k] = low[k // 2][k % 2].astype(F32)

    acc = keep[...] + recv[...].astype(F32)
    for ky in range(4):
        for kz in range(2):
            n = ((y + 4 - ky) % 4) * 2 + (zh ^ kz)
            left = pltpu.roll(ranks[narrow ^ n], (4 - x) % 4 * per, 1).astype(BF16)
            acc = acc + contract(left, side[ky][kz].reshape(4 * per, -1), 1, 0)
    out[...] = acc.astype(BF16)


def end(where, keep, recv, low, side):
    rows = keep.shape[0]
    _, _, per, width = side[0].shape
    tile = 512 if width % 512 == 0 else width
    column = pl.BlockSpec((rows, tile), lambda i, where: (0, i))
    block = pl.BlockSpec((2, 4, per, tile), lambda i, where: (0, 0, 0, i))
    return call(
        end_body,
        where,
        width // tile,
        [keep, recv, *low, *side],
        [column, column] + [whole(u) for u in low] + [block] * 4,
        [jax.ShapeDtypeStruct((rows, width), BF16)],
        [column],
        [pltpu.VMEM((8, rows, 4 * per), F32)],
        64 * rows * per * width,
    )[0]


def shards(
    tokens,
    routing,
    gate_shared,
    up_shared,
    down_shared,
    gate_in,
    gate_out,
    up_in,
    up_out,
    down_in,
    down_out,
):
    wide, narrow = lax.axis_index("wide"), lax.axis_index("narrow")
    y, zh, x = wide // 8, wide // 4 % 2, wide % 4
    zl, core = narrow // 2, narrow % 2

    def where(half, side=0):
        return jnp.stack([half, core, zl, y, zh, x, narrow, core * 0 + side]).astype(jnp.int32)

    mixing = routing.astype(F32) / 1024.0
    rows, width = tokens.shape
    hid = gate_shared.shape[1]
    experts, per = gate_in.shape[1:]
    half = rows // 2
    chunk = rows * 4

    def turned(factor):
        return jnp.transpose(factor, (1, 2, 0))

    def scaled(factor):
        flat = factor.astype(F32) * mixing[:, None, None]
        return flat.astype(BF16).reshape(experts * per, width)

    def by_rank(factor):
        cut = factor.reshape(experts, 4, per, hid)
        return jnp.transpose(cut, (1, 0, 2, 3)).reshape(4 * experts * per, hid)

    down_own = scaled(turned(down_out))
    other = swap_zh(jnp.concatenate([tokens, down_own]))
    down_pair = jnp.stack([down_own, other[rows:]])
    other = other[:rows]
    both = jnp.where(zh == 0, jnp.stack([tokens, other]), jnp.stack([other, tokens]))
    part_a = gather4(both[:, :half], send_x, x).reshape(chunk, width)
    part_b = gather4(both[:, half:], send_y, y).reshape(chunk, width)
    side = jnp.concatenate([scaled(turned(gate_in)), scaled(turned(up_in))])
    part_a, part_b, side, down_pair = lax.optimization_barrier((part_a, part_b, side, down_pair))
    toks_a = pieces4(part_a, send_y)
    toks_b = pieces4(part_b, send_x)

    out_g, out_u, _ = lax.optimization_barrier((gate_out, up_out, other))
    hid_own = pad_rows(jnp.stack([by_rank(out_g).T, by_rank(out_u).T]))
    hid_fac = lax.all_gather(hid_own, "narrow")
    weight = pad_rows(jnp.concatenate([down_shared, by_rank(down_in).T], axis=1))

    low_give, low_keep = low_rank(where(core), toks_a, toks_b, side)
    low_recv = swap_n(low_give, 1)

    def joined(a, b, slot):
        return a[slot].astype(F32) + b[slot].astype(F32)

    args = (toks_a, toks_b, gate_shared.T, up_shared.T)
    give = first(after(where(1 - core, 1), low_give), *args)
    recv = swap_n(give, 1)
    low = joined(low_keep, low_recv, 0)
    for k in (3, 2, 1):
        low = low + swap_n(joined(low_keep, low_recv, k).astype(BF16), 2 * k).astype(F32)
    low = low.astype(BF16)
    keep = first(where(core, 1), *args)
    low_other = swap_zh(low)
    cross_in = joined(keep, recv, 0).astype(BF16)

    def line(pair):
        return jnp.stack([pair] + [send_x(pair, 4 - m) for m in (1, 2, 3)], axis=1)

    cross = swap_n(after(cross_in, low_other), 2)

    give = first(after(where(1 - core, 0), cross_in), *args)
    near_recv = swap_n(give, 1)
    near_keep = first(after(where(core, 0), give), *args)
    far = (joined(keep, recv, 1) + cross.astype(F32)).astype(BF16)
    near = swap_n(after(joined(near_keep, near_recv, 0).astype(BF16), cross), 2)
    got = [near, swap_n(far, 4)]

    low_line = line(jnp.stack([low, low_other]))
    low = pieces4(low_line, send_y)
    down_line = line(after(down_pair, far, low_line))
    down_side = [down_line, send_y(down_line, 1), None, send_y(down_line, 3)]
    near_keep = after(near_keep, down_side[1], down_side[3])
    hidden = middle(where(core), near_keep, near_recv, got, hid_fac, low, hid)
    down_side[2] = send_y(after(down_line, hidden), 2)

    column = [hidden] + [swap_n(hidden, 2 * k) for k in (1, 2, 3)]
    sibling = [swap_n(piece, 1) for piece in column]

    column[0] = after(column[0], down_side[2])
    out_a, out_b = last(where(core), column, sibling, weight)
    out_a = [out_a[0]] + [send_y(out_a[k], k) for k in (1, 2, 3)]
    out_b = [out_b[0]] + [send_x(out_b[k], k) for k in (1, 2, 3)]
    out_a, out_b = split(where(core), out_a, out_b)
    out_a = [out_a[0]] + [send_x(out_a[k], k) for k in (1, 2, 3)]
    out_b = [out_b[0]] + [send_y(out_b[k], k) for k in (1, 2, 3)]
    kept, give = halve(where(core), out_a, out_b)
    recv = swap_zh(give)
    mine = (kept[:, width:] + recv[:, width:].astype(F32)).astype(BF16)
    mine = jnp.stack([mine, swap_n(mine, 1)])
    ranks = [mine] + [swap_n(mine, 2 * k) for k in (1, 2, 3)]
    return end(where(core), kept, recv, ranks, down_side)


def solution(mesh):
    return jax.shard_map(
        shards,
        mesh=mesh,
        in_specs=(
            P("wide", "narrow"),
            P(),
            P("narrow", "wide"),
            P("narrow", "wide"),
            P("wide", "narrow"),
            P("narrow", None, "wide"),
            P(None, "narrow", "wide"),
            P("narrow", None, "wide"),
            P(None, "narrow", "wide"),
            P(None, "narrow", "wide"),
            P("narrow", None, "wide"),
        ),
        out_specs=P("wide", "narrow"),
        check_vma=False,
    )
```

```python
import functools

import jax
import jax.numpy as jnp
from jax import lax
from jax.experimental import pallas as pl
from jax.experimental.pallas import tpu as pltpu
from jax.sharding import PartitionSpec as P

AXES = ("wide", "narrow")
F32, BF16 = jnp.float32, jnp.bfloat16
VMEM_LIMIT = 14 * 1024 * 1024


def pairs(move):
    table = []
    for wide in range(32):
        y, zh, x = wide // 8, wide // 4 % 2, wide % 4
        for narrow in range(8):
            ty, tzh, tx, tn = move(y, zh, x, narrow)
            table.append((wide * 8 + narrow, ((ty * 2 + tzh) * 4 + tx) * 8 + tn))
    return table


def send_x(a, k):
    return lax.ppermute(a, AXES, pairs(lambda y, zh, x, n: (y, zh, (x + k) % 4, n)))


def send_y(a, k):
    return lax.ppermute(a, AXES, pairs(lambda y, zh, x, n: ((y + k) % 4, zh, x, n)))


def swap_zh(a):
    return lax.ppermute(a, AXES, pairs(lambda y, zh, x, n: (y, 1 - zh, x, n)))


def swap_n(a, k):
    return lax.ppermute(a, AXES, pairs(lambda y, zh, x, n: (y, zh, x, n ^ k)))


def after(a, *others):
    return lax.optimization_barrier((a,) + others)[0]


def gather4(own, send, at):
    got = [own] + [send(own, 4 - m) for m in (1, 2, 3)]
    ring = jnp.stack(got + got[:3])
    return lax.dynamic_slice_in_dim(ring, (4 - at) % 4, 4, 0)


def pieces4(own, send):
    return [own] + [send(own, k) for k in (1, 2, 3)]


def pick(a, at):
    return lax.dynamic_index_in_dim(a, at, 0, keepdims=False)


def contract(a, b, da, db):
    return lax.dot_general(a, b, (((da,), (db,)), ((), ())), preferred_element_type=F32)


def padded(rows, unit=16):
    return (rows + unit - 1) // unit * unit


def pad_rows(a, unit=16):
    rows = a.shape[-2]
    return jnp.pad(a, [(0, 0)] * (a.ndim - 2) + [(0, padded(rows, unit) - rows), (0, 0)])


def whole(a):
    zeros = (0,) * a.ndim
    return pl.BlockSpec(a.shape, lambda i, where: zeros)


HERE = pl.BlockSpec(memory_space=pl.ANY)


def in_hbm(arrays):
    return [pltpu.with_memory_space_constraint(a, pltpu.HBM) for a in arrays]


def call(body, where, grid, ins, in_specs, outs, out_specs, scratch, flops):
    moved = sum(a.size * a.dtype.itemsize for a in list(ins) + list(outs))
    return pl.pallas_call(
        body,
        out_shape=outs,
        grid_spec=pltpu.PrefetchScalarGridSpec(
            num_scalar_prefetch=1,
            grid=(grid,),
            in_specs=in_specs,
            out_specs=out_specs,
            scratch_shapes=scratch,
        ),
        compiler_params=pltpu.CompilerParams(vmem_limit_bytes=VMEM_LIMIT),
        cost_estimate=pl.CostEstimate(flops=flops, bytes_accessed=moved, transcendentals=0),
    )(where, *ins)


def fetch(where, half, a, b, toks, sems, slot_of):
    pos = jnp.where(half == 0, where[3], where[5])
    chunk = a[0].shape[0]
    for k in range(4):
        slot, wanted = slot_of(((pos + 4 - k) % 4) ^ where[2])
        rows = toks.at[pl.ds(pl.multiple_of(slot * chunk, chunk), chunk), :]
        for at, pieces in ((0, a), (1, b)):

            @pl.when((half == at) & wanted)
            def _():
                pltpu.make_async_copy(pieces[k], rows, sems.at[slot]).start()


def arrived(a, toks, sems, slots):
    chunk = a[0].shape[0]
    for slot in range(slots):
        rows = toks.at[pl.ds(slot * chunk, chunk), :]
        pltpu.make_async_copy(a[0], rows, sems.at[slot]).wait()


def low_body(where, *refs):
    a, b = refs[:4], refs[4:8]
    side, give, keep, toks, sems = refs[8:]
    chunk = a[0].shape[0]
    halves = ((1 - where[1], give, 0), (where[1], keep, 4))
    for half, _, base in halves:
        fetch(where, half, a, b, toks, sems, lambda near: (near + base, True))
    arrived(a, toks, sems, 8)
    for _, out, base in halves:
        rows = slice(base * chunk, (base + 4) * chunk)
        sums = contract(side[...], toks[rows, :], 1, 1)
        for k in range(4):
            out[k] = sums[:, k * chunk : (k + 1) * chunk].astype(BF16)


def low_rank(where, a, b, side):
    chunk, width = a[0].shape
    out = jax.ShapeDtypeStruct((4, side.shape[0], chunk), BF16)
    return call(
        low_body,
        where,
        1,
        [*a, *b, side],
        [HERE] * 8 + [whole(side)],
        [out, out],
        [whole(out), whole(out)],
        [pltpu.VMEM((8 * chunk, width), BF16), pltpu.SemaphoreType.DMA((8,))],
        16 * side.shape[0] * width * chunk,
    )


def first_body(where, *refs):
    a, b = refs[:4], refs[4:8]
    gate, up, out, toks, sems = refs[8:]
    chunk = a[0].shape[0]

    @pl.when(pl.program_id(0) == 0)
    def _():
        fetch(where, where[0], a, b, toks, sems, lambda near: (1 - near % 2, near // 2 == where[7]))
        arrived(a, toks, sems, 2)

    for g, weight in enumerate((gate, up)):
        sums = contract(weight[...], toks[...], 1, 1)
        for slot in range(2):
            out[slot, g] = sums[:, slot * chunk : (slot + 1) * chunk].astype(BF16)


def first(where, a, b, gate, up):
    hid, width = gate.shape
    chunk = a[0].shape[0]
    tile = 464
    weight = pl.BlockSpec((tile, width), lambda i, where: (i, 0))
    return call(
        first_body,
        where,
        pl.cdiv(hid, tile),
        [*a, *b, gate, up],
        [HERE] * 8 + [weight, weight],
        [jax.ShapeDtypeStruct((2, 2, padded(hid), chunk), BF16)],
        [pl.BlockSpec((2, 2, tile, chunk), lambda i, where: (0, 0, i, 0))],
        [pltpu.VMEM((2 * chunk, width), BF16), pltpu.SemaphoreType.DMA((2,))],
        8 * hid * width * chunk,
    )[0]


def arrange(where, blocks, store):
    y, zh, x = where[3], where[4], where[5]
    for ky in range(4):
        for kz in range(2):
            n = ((y + 4 - ky) % 4) * 2 + (zh ^ kz)
            for kx in range(4):
                store(n, (x + kx) % 4, blocks[ky][kz, kx])


def mid_body(hid, where, *refs):
    keep, recv = refs[:2]
    got, fac, low = refs[2:4], refs[4], refs[5:9]
    out, ranks = refs[9:]
    per = ranks.shape[3]

    @pl.when(pl.program_id(0) == 0)
    def _():
        def store(n, xs, block):
            for g in range(2):
                ranks[g, n, xs] = block[g * per : (g + 1) * per, :]

        arrange(where, low, store)

    values = []
    for g in range(2):
        acc = keep[0, g].astype(F32) + recv[0, g].astype(F32)
        for part in got:
            acc = acc + part[g].astype(F32)
        side = jnp.concatenate([fac[k, g] for k in range(8)], axis=1)
        values.append(acc + contract(side, ranks[g].reshape(-1, ranks.shape[4]), 1, 0))
    gate, up = values
    value = gate / (1.0 + jnp.exp(-gate)) * up
    row = pl.program_id(0) * out.shape[0] + lax.broadcasted_iota(jnp.int32, value.shape, 0)
    out[...] = jnp.where(row < hid, value, 0.0).astype(BF16)


def middle(where, keep, recv, got, fac, low, used):
    _, _, hid, chunk = keep.shape
    tile = 256
    full = pl.BlockSpec((1, 2, tile, chunk), lambda i, where: (1, 0, i, 0))
    part = pl.BlockSpec((2, tile, chunk), lambda i, where: (0, i, 0))
    factor = pl.BlockSpec((8, 2, tile, fac.shape[3]), lambda i, where: (0, 0, i, 0))
    return call(
        functools.partial(mid_body, used),
        where,
        pl.cdiv(hid, tile),
        [*in_hbm([keep, recv]), *got, *in_hbm([fac]), *low],
        [full, full] + [part] * 2 + [factor] + [whole(p) for p in low],
        [jax.ShapeDtypeStruct((hid, chunk), BF16)],
        [pl.BlockSpec((tile, chunk), lambda i, where: (i, 0))],
        [pltpu.VMEM((2, 8, 4, low[0].shape[2] // 2, chunk), BF16)],
        32 * fac.shape[3] * hid * chunk,
    )[0]


def last_body(where, *refs):
    own, sib, weight = refs[:4], refs[4:8], refs[8]
    outs, hidden, sems = refs[9:17], refs[17], refs[18]
    core, zl = where[1], where[2]
    chunk = hidden.shape[2]

    @pl.when(pl.program_id(0) == 0)
    def _():
        copies = []
        for at, pieces in ((core, own), (1 - core, sib)):
            pos = jnp.where(at == 0, where[3], where[5])
            for k in range(4):
                slot = hidden.at[at * 4 + ((zl ^ k) + 4 - pos) % 4]
                copies.append(pltpu.make_async_copy(pieces[k], slot, sems.at[len(copies)]))
                copies[-1].start()
        for copy in copies:
            copy.wait()

    left = jnp.concatenate([hidden[k] for k in range(8)], axis=1)
    sums = contract(left, weight[...], 0, 0)
    for k in range(8):
        outs[k][...] = sums[k * chunk : (k + 1) * chunk].astype(BF16)


def last(where, own, sib, weight):
    hid, chunk = own[0].shape
    cols = weight.shape[1]
    tile = 384 if cols % 384 == 0 else cols
    outs = call(
        last_body,
        where,
        cols // tile,
        [*own, *sib, weight],
        [HERE] * 8 + [pl.BlockSpec((hid, tile), lambda i, where: (0, i))],
        [jax.ShapeDtypeStruct((chunk, cols), BF16)] * 8,
        [pl.BlockSpec((chunk, tile), lambda i, where: (0, i))] * 8,
        [pltpu.VMEM((8, hid, chunk), BF16), pltpu.SemaphoreType.DMA((8,))],
        16 * chunk * hid * cols,
    )
    return outs[:4], outs[4:]


def add4(parts, rows):
    acc = parts[0][rows, :].astype(F32)
    for part in parts[1:]:
        acc = acc + part[rows, :].astype(F32)
    return acc


def split_body(where, *refs):
    size = refs[8].shape[0]
    for parts, outs, pos in ((refs[:4], refs[8:12], where[5]), (refs[4:8], refs[12:16], where[3])):
        for k in range(4):
            start = pl.multiple_of((pos + k) % 4 * size, size)
            outs[k][...] = add4(parts, pl.ds(start, size)).astype(BF16)


def split(where, a, b):
    rows, cols = a[0].shape
    outs = [jax.ShapeDtypeStruct((rows // 4, cols), BF16)] * 8
    outs = call(split_body, where, 1, [*a, *b], [whole(p) for p in [*a, *b]], outs, [whole(p) for p in outs], [], 0)
    return outs[:4], outs[4:]


def halve_body(where, *refs):
    keep, give = refs[8:]
    size = keep.shape[0] // 2
    for h in range(2):
        parts = refs[4 * h : 4 * h + 4]
        for out, at in ((keep, where[4]), (give, 1 - where[4])):
            start = pl.multiple_of(at * size, size)
            out[h * size : (h + 1) * size, :] = add4(parts, pl.ds(start, size)).astype(out.dtype)


def halve(where, a, b):
    outs = [jax.ShapeDtypeStruct(a[0].shape, F32), jax.ShapeDtypeStruct(a[0].shape, BF16)]
    return call(halve_body, where, 1, [*a, *b], [whole(p) for p in [*a, *b]], outs, [whole(p) for p in outs], [], 0)


def end_body(where, *refs):
    keep, recv, low, side = refs[0], refs[1], refs[2:6], refs[6:10]
    out, ranks = refs[10:]
    y, zh, x, narrow = where[3], where[4], where[5], where[6]
    per = side[0].shape[2]

    @pl.when(pl.program_id(0) == 0)
    def _():
        for k in range(8):
            ranks[k] = low[k // 2][k % 2].astype(F32)

    acc = keep[...] + recv[...].astype(F32)
    for ky in range(4):
        for kz in range(2):
            n = ((y + 4 - ky) % 4) * 2 + (zh ^ kz)
            left = pltpu.roll(ranks[narrow ^ n], (4 - x) % 4 * per, 1).astype(BF16)
            acc = acc + contract(left, side[ky][kz].reshape(4 * per, -1), 1, 0)
    out[...] = acc.astype(BF16)


def end(where, keep, recv, low, side):
    rows = keep.shape[0]
    _, _, per, width = side[0].shape
    tile = 512 if width % 512 == 0 else width
    column = pl.BlockSpec((rows, tile), lambda i, where: (0, i))
    block = pl.BlockSpec((2, 4, per, tile), lambda i, where: (0, 0, 0, i))
    return call(
        end_body,
        where,
        width // tile,
        [keep, recv, *low, *side],
        [column, column] + [whole(u) for u in low] + [block] * 4,
        [jax.ShapeDtypeStruct((rows, width), BF16)],
        [column],
        [pltpu.VMEM((8, rows, 4 * per), F32)],
        64 * rows * per * width,
    )[0]


def shards(
    tokens,
    routing,
    gate_shared,
    up_shared,
    down_shared,
    gate_in,
    gate_out,
    up_in,
    up_out,
    down_in,
    down_out,
):
    wide, narrow = lax.axis_index("wide"), lax.axis_index("narrow")
    y, zh, x = wide // 8, wide // 4 % 2, wide % 4
    zl, core = narrow // 2, narrow % 2

    def where(half, side=0):
        return jnp.stack([half, core, zl, y, zh, x, narrow, core * 0 + side]).astype(jnp.int32)

    mixing = routing.astype(F32) / 1024.0
    rows, width = tokens.shape
    hid = gate_shared.shape[1]
    experts, per = gate_in.shape[1:]
    half = rows // 2
    chunk = rows * 4

    def turned(factor):
        return jnp.transpose(factor, (1, 2, 0))

    def scaled(factor):
        flat = factor.astype(F32) * mixing[:, None, None]
        return flat.astype(BF16).reshape(experts * per, width)

    def by_rank(factor):
        cut = factor.reshape(experts, 4, per, hid)
        return jnp.transpose(cut, (1, 0, 2, 3)).reshape(4 * experts * per, hid)

    down_own = scaled(turned(down_out))
    other = swap_zh(jnp.concatenate([tokens, down_own]))
    down_pair = jnp.stack([down_own, other[rows:]])
    other = other[:rows]
    both = jnp.where(zh == 0, jnp.stack([tokens, other]), jnp.stack([other, tokens]))
    part_a = gather4(both[:, :half], send_x, x).reshape(chunk, width)
    part_b = gather4(both[:, half:], send_y, y).reshape(chunk, width)
    side = jnp.concatenate([scaled(turned(gate_in)), scaled(turned(up_in))])
    part_a, part_b, side, down_pair = lax.optimization_barrier((part_a, part_b, side, down_pair))
    toks_a = pieces4(part_a, send_y)
    toks_b = pieces4(part_b, send_x)

    out_g, out_u, _ = lax.optimization_barrier((gate_out, up_out, other))
    hid_own = pad_rows(jnp.stack([by_rank(out_g).T, by_rank(out_u).T]))
    hid_fac = lax.all_gather(hid_own, "narrow")
    weight = pad_rows(jnp.concatenate([down_shared, by_rank(down_in).T], axis=1))

    low_give, low_keep = low_rank(where(core), toks_a, toks_b, side)
    low_recv = swap_n(low_give, 1)

    def joined(a, b, slot):
        return a[slot].astype(F32) + b[slot].astype(F32)

    args = (toks_a, toks_b, gate_shared.T, up_shared.T)
    give = first(after(where(1 - core, 1), low_give), *args)
    recv = swap_n(give, 1)
    low = joined(low_keep, low_recv, 0)
    for k in (3, 2, 1):
        low = low + swap_n(joined(low_keep, low_recv, k).astype(BF16), 2 * k).astype(F32)
    low = low.astype(BF16)
    keep = first(where(core, 1), *args)
    low_other = swap_zh(low)
    cross_in = joined(keep, recv, 0).astype(BF16)

    def line(pair):
        return jnp.stack([pair] + [send_x(pair, 4 - m) for m in (1, 2, 3)], axis=1)

    cross = swap_n(after(cross_in, low_other), 2)

    give = first(after(where(1 - core, 0), cross_in), *args)
    near_recv = swap_n(give, 1)
    near_keep = first(after(where(core, 0), give), *args)
    far = (joined(keep, recv, 1) + cross.astype(F32)).astype(BF16)
    near = swap_n(after(joined(near_keep, near_recv, 0).astype(BF16), cross), 2)
    got = [near, swap_n(far, 4)]

    low_line = line(jnp.stack([low, low_other]))
    low = pieces4(low_line, send_y)
    down_line = line(after(down_pair, far))
    down_side = [down_line, send_y(down_line, 1), None, send_y(down_line, 3)]
    near_keep = after(near_keep, down_side[1], down_side[3])
    hidden = middle(where(core), near_keep, near_recv, got, hid_fac, low, hid)
    down_side[2] = send_y(after(down_line, hidden), 2)

    column = [hidden] + [swap_n(hidden, 2 * k) for k in (1, 2, 3)]
    sibling = [swap_n(piece, 1) for piece in column]

    column[0] = after(column[0], down_side[2])
    out_a, out_b = last(where(core), column, sibling, weight)
    out_a = [out_a[0]] + [send_y(out_a[k], k) for k in (1, 2, 3)]
    out_b = [out_b[0]] + [send_x(out_b[k], k) for k in (1, 2, 3)]
    out_a, out_b = split(where(core), out_a, out_b)
    out_a = [out_a[0]] + [send_x(out_a[k], k) for k in (1, 2, 3)]
    out_b = [out_b[0]] + [send_y(out_b[k], k) for k in (1, 2, 3)]
    kept, give = halve(where(core), out_a, out_b)
    recv = swap_zh(give)
    mine = (kept[:, width:] + recv[:, width:].astype(F32)).astype(BF16)
    mine = jnp.stack([mine, swap_n(mine, 1)])
    ranks = [mine] + [swap_n(mine, 2 * k) for k in (1, 2, 3)]
    return end(where(core), kept, recv, ranks, down_side)


def solution(mesh):
    return jax.shard_map(
        shards,
        mesh=mesh,
        in_specs=(
            P("wide", "narrow"),
            P(),
            P("narrow", "wide"),
            P("narrow", "wide"),
            P("wide", "narrow"),
            P("narrow", None, "wide"),
            P(None, "narrow", "wide"),
            P("narrow", None, "wide"),
            P(None, "narrow", "wide"),
            P(None, "narrow", "wide"),
            P("narrow", None, "wide"),
        ),
        out_specs=P("wide", "narrow"),
        check_vma=False,
    )
```
